32 devices in a mesh: groups: 2 (over x), expert: 4 (over y, core), dp: 4 (over z).
Axes of the slice: x: 2, y: 2, z: 4, core: 2. Of those that a mesh axis runs over, the one named last changes fastest.
Arguments:
- tokens: bfloat16 [4096, 2048], P(('groups', 'expert', 'dp')), parts along dimension 0, may hold values from -6 to 6
- route_ids: int32 [4096, 2], P(('groups', 'expert', 'dp')), parts along dimension 0, may hold values from 0 to 3, all different within a row; in each aligned block of 128 rows (0 to 127, 128 to 255, ...) at most 128 rows name the same one
- route_probs: bfloat16 [4096, 2], P(('groups', 'expert', 'dp')), parts along dimension 0, may hold values from 0.049804688 to 1
- cotangent: bfloat16 [4096, 2048], P(('groups', 'expert', 'dp')), parts along dimension 0, may hold values from -6 to 6
- w_gate_up: bfloat16 [4, 2, 384, 2048], P('expert', None, 'dp'), may hold values from -0.125 to 0.125
- w_down: bfloat16 [4, 384, 2048], P('expert', 'dp'), may hold values from -0.3125 to 0.3125
Outputs:
- grad_tokens: bfloat16 [4096, 2048], P(('groups', 'expert', 'dp')), parts along dimension 0
- grad_gate_up: float32 [8, 2, 384, 2048], P(('groups', 'expert'), None, 'dp'), parts along dimension 0
- grad_down: float32 [8, 384, 2048], P(('groups', 'expert'), 'dp'), parts along dimension 0
The draws below stay inside these ranges and needn't reach their ends.
There are 2 independent parts, one for each index of `groups`. The reference program is written for one: setup_inputs(seed, part) draws one part's arguments, and reference() takes and returns one part's arrays. A program takes and returns all parts, laid end to end along the dimension named above; an argument that names none is the same for every part. Nothing has to cross between parts.
Inputs may be any that keep to these rules, and one draw needn't show every extreme that they name: `route_ids`: each row names 2 different experts; among the 128 rows of one device no expert is named by more than 128 rows.
All inputs are finite; a program needn't handle non-finite values.
Results may differ from the reference program's by a relative error of at most 0.0095.
Values may be sent and summed in bfloat16 or wider, within the bound.
No kernel may reach another device: no remote copies, remote signals or barrier semaphores. Data moves between devices by JAX's collectives and lax.ppermute only.
A program may use at most 128 MiB of HBM per device.

```python
import math
import jax
import jax.numpy as jnp
import numpy as np
from jax import lax

D = 2048
FH = 384
TOK_DEV = 128
EXPERTS = 4
TOPK = 2
MOST = 128
TOKENS = 2048
N_EXPERT = 4
N_DP = 4


def block_scale(own_key, shape, split, least, high):
    loudness = 1.0
    for dim, blocks in split:
        heights = jax.random.uniform(jax.random.fold_in(jax.random.fold_in(own_key, 6), dim), (blocks,), jnp.float32, least / len(split), high / len(split))
        loudness = loudness * jnp.repeat(jnp.exp(heights), shape[dim] // blocks).reshape((-1,) + (1,) * (len(shape) - 1 - dim))
    return loudness


def assign_block(rng, own, number, rows, count, top, most, skew):
    order = jax.random.permutation(rng, count)
    crowded, usual = portions_of(count, rows * top, most, skew, True), portions_of(count, rows * top, most, skew, False)
    places = jnp.arange(count)

    def named(tallies, turn):
        used = int((tallies > 0).sum())
        fixed = max(1, used // 4)
        passed = fixed + (places - fixed + turn * (used - fixed)) % max(1, count - fixed)
        return jnp.zeros((count,), jnp.int32).at[order[jnp.where(places < fixed, places, passed)]].set(jnp.asarray(tallies, jnp.int32))

    tallies = jnp.where(number % 4 == 0, named(crowded, number // 4), named(usual, number - number // 4 - 1))
    mixed = jax.random.permutation(jax.random.fold_in(own, 3), count)
    donor, taker = mixed[0:count // 2 * 2:2], mixed[1:count // 2 * 2:2]
    room = jnp.minimum(tallies[donor] - 1, most - tallies[taker]) // 2
    room = jnp.where((donor == order[0]) | (taker == order[0]) | (tallies[taker] == 0), 0, jnp.maximum(room, 0))
    passed = jax.random.randint(jax.random.fold_in(own, 4), (count // 2,), 0, 1 << 20) % (room + 1)
    tallies = tallies.at[donor].add(-passed).at[taker].add(passed)
    labels = jnp.searchsorted(jnp.cumsum(tallies), jnp.arange(rows * top), side="right").astype(jnp.int32)
    table = labels.reshape(top, rows).T
    table = table[jax.random.permutation(jax.random.fold_in(own, 1), rows)]
    turn = jax.random.randint(jax.random.fold_in(own, 2), (rows, 1), 0, top)
    return jnp.take_along_axis(table, (jnp.arange(top)[None, :] + turn) % top, axis=1)


def portions_of(number_of, total, bound, slope, full):
    portions = [(1 << 20) // math.isqrt(grade ** slope) + 1 for grade in range(1, number_of + 1)]
    largest = bound if full else min(bound, max(-(-total // number_of), total * portions[0] // sum(portions)))
    least = 1 if total - largest >= number_of - 1 else 0
    counts, spare = [largest] + [least] * (number_of - 1), total - largest - least * (number_of - 1)
    while spare > 0:
        free = [i for i in range(1, number_of) if counts[i] < largest] or [i for i in range(1, number_of) if counts[i] < bound]
        mass, remaining = sum([portions[i] for i in free]), spare
        for i in free:
            more = min(bound - counts[i], max(1, remaining * portions[i] // mass), spare)
            counts[i] = counts[i] + more
            spare = spare - more
    return np.array(counts)


def centred(own_key, dims, spread, bound, split=(), kind=jnp.bfloat16):
    loudness = block_scale(own_key, dims, split, -0.22, 0.18) if split else 1.0
    result = jax.random.normal(own_key, dims, jnp.float32) * spread * loudness
    return jnp.minimum(jnp.maximum(result, -bound), bound).astype(kind)


def setup_inputs(seed: int = 0, part: int = 0) -> dict:
    streams_of = jax.random.split(jax.random.key(seed), 7)
    own_keys = jax.random.split(jax.random.fold_in(streams_of[6], part), 7)
    tokens = centred(own_keys[0], (TOKENS, D), 1.0, 6.0, ((0, 16),))
    route_ids_keys = jax.random.split(jax.random.fold_in(own_keys[1], 1), TOKENS // TOK_DEV)
    route_ids_turns = jax.random.permutation(jax.random.fold_in(own_keys[1], 3), TOKENS // TOK_DEV)
    route_ids = jax.vmap(lambda own, number: assign_block(jax.random.fold_in(own_keys[1], 2), own, number, TOK_DEV, EXPERTS, TOPK, MOST, 2))(route_ids_keys, route_ids_turns).reshape((TOKENS, TOPK))
    route_probs = jnp.clip(jnp.exp(math.log(1.0) - 2.9996462 * jax.random.uniform(own_keys[2], (TOKENS, TOPK), jnp.float32) ** block_scale(own_keys[2], (TOKENS, TOPK), ((0, 16),), -0.2, 0.2)), 0.049804688, 1.0).astype(jnp.bfloat16)
    cotangent = centred(own_keys[3], (TOKENS, D), 1.0, 6.0, ((0, 16),))
    w_gate_up = centred(streams_of[4], (EXPERTS, 2, FH, D), D ** -0.5, 0.125, ((0, 4), (2, 4)))
    w_down = centred(streams_of[5], (EXPERTS, FH, D), FH ** -0.5, 0.3125, ((0, 4), (1, 4)))
    return dict(tokens=tokens, route_ids=route_ids, route_probs=route_probs, cotangent=cotangent, w_gate_up=w_gate_up, w_down=w_down)


def reference(tokens, route_ids, route_probs, cotangent, w_gate_up, w_down):
    group_rows = TOK_DEV * N_DP
    slot_count = N_DP * MOST
    hid_block = FH // N_DP
    pair_index = jnp.arange(group_rows * TOPK, dtype=jnp.int32)

    def per_group(carry, inputs):
        sum_gate_up, sum_down = carry
        group_x, group_ids, group_probs, group_dy = inputs
        flat_ids = group_ids.reshape(-1)
        flat_probs = group_probs.reshape(-1).astype(jnp.float32)

        def per_expert(accum, expert):
            mask = flat_ids == expert
            position = jnp.cumsum(mask.astype(jnp.int32)) - 1
            target = jnp.where(mask, position, slot_count).astype(jnp.int32)
            slot_rows = jnp.zeros((slot_count,), jnp.int32).at[target].set(pair_index // TOPK, mode="drop")
            slot_weight = jnp.zeros((slot_count,), jnp.float32).at[target].set(flat_probs, mode="drop")
            rows_in = group_x[slot_rows].astype(jnp.float32)
            rows_back = group_dy[slot_rows].astype(jnp.float32)
            gate_up = w_gate_up[expert].astype(jnp.float32)
            down = w_down[expert].astype(jnp.float32)
            projected = jnp.einsum("sd,chd->csh", rows_in, gate_up)
            gate_act = projected[0]
            up_act = projected[1]
            sigma = jax.nn.sigmoid(gate_act)
            silu_gate = gate_act * sigma
            weighted = (slot_weight[:, None] * silu_gate * up_act).astype(jnp.bfloat16)
            back_hidden = slot_weight[:, None] * jnp.einsum("sd,hd->sh", rows_back, down)
            gate_grad = (back_hidden * up_act * sigma * (1.0 + gate_act * (1.0 - sigma))).astype(jnp.bfloat16)
            up_grad = (back_hidden * silu_gate).astype(jnp.bfloat16)
            both = jnp.stack([gate_grad, up_grad]).astype(jnp.float32)
            part_down = jnp.einsum("sh,sd->hd", weighted.astype(jnp.float32), rows_back).astype(jnp.bfloat16)
            part_gate_up = jnp.einsum("csh,sd->chd", both, rows_in).astype(jnp.bfloat16)
            blocked = both.reshape(2, slot_count, N_DP, hid_block)
            blocked_weight = gate_up.reshape(2, N_DP, hid_block, D)
            contrib = jnp.einsum("csnh,cnhd->nsd", blocked, blocked_weight)
            accum = accum.at[:, slot_rows].add(contrib)
            return accum, (part_gate_up, part_down)

        accum, parts = lax.scan(per_expert, jnp.zeros((N_DP, group_rows, D), jnp.float32),
                                jnp.arange(EXPERTS, dtype=jnp.int32))
        parts_gate_up, parts_down = parts
        rounded = lax.optimization_barrier(accum.astype(jnp.bfloat16))
        group_grad = jnp.sum(rounded.astype(jnp.float32), axis=0).astype(jnp.bfloat16)
        new_carry = (sum_gate_up + parts_gate_up.astype(jnp.float32), sum_down + parts_down.astype(jnp.float32))
        return new_carry, group_grad

    start = (jnp.zeros((EXPERTS, 2, FH, D), jnp.float32), jnp.zeros((EXPERTS, FH, D), jnp.float32))
    inputs = (tokens.reshape(N_EXPERT, group_rows, D), route_ids.reshape(N_EXPERT, group_rows, TOPK),
              route_probs.reshape(N_EXPERT, group_rows, TOPK), cotangent.reshape(N_EXPERT, group_rows, D))
    sums, grad_rows = lax.scan(per_group, start, inputs)
    grad_gate_up, grad_down = sums
    return grad_rows.reshape(TOKENS, D), grad_gate_up, grad_down
```

```python
import jax
import jax.numpy as jnp
from jax import lax
from jax.sharding import PartitionSpec as P


def ring_pairs(count):
    order = [0] + list(range(1, count, 2)) + list(range(2, count, 2))[::-1]
    return [(order[i], order[(i + 1) % count]) for i in range(count)]


def onward(block):
    return lax.ppermute(block, "dp", ring_pairs(lax.axis_size("dp")))


def swapped(block, bit):
    return lax.ppermute(block, "expert", [(i, i ^ bit) for i in range(lax.axis_size("expert"))])


def bits_of(count):
    return [1 << i for i in range(count.bit_length() - 1)]


def all_experts(block):
    held = {0: block}
    for bit in bits_of(lax.axis_size("expert"))[::-1]:
        held.update({k | bit: swapped(v, bit) for k, v in list(held.items())})
    return [held[k] for k in range(len(held))]


def summed_to_owner(terms):
    left = {k: v for k, v in enumerate(terms)}
    for bit in bits_of(len(terms)):
        stay = [k for k in left if not k & bit]
        got = {k: swapped(left[k | bit], bit) for k in stay[::-1]}
        left = {k: left[k].astype(jnp.float32) + got[k].astype(jnp.float32) for k in stay}
        if len(left) > 1:
            left = {k: v.astype(jnp.bfloat16) for k, v in left.items()}
    return left[0]


def f32_dot(spec, a, b):
    return jnp.einsum(spec, a, b, preferred_element_type=jnp.float32)


def hidden_terms(x, dy, prob, gate, up, down):
    gate_act = f32_dot("rd,hd->rh", x, gate)
    up_act = f32_dot("rd,hd->rh", x, up)
    back = f32_dot("rd,hd->rh", dy, down)
    hid = gate.shape[0] // prob.shape[0]
    weight = jnp.repeat(prob.T.astype(jnp.float32), hid, axis=1)
    sigma = jax.nn.sigmoid(gate_act)
    silu_gate = gate_act * sigma
    weighted = (weight * silu_gate * up_act).astype(jnp.bfloat16)
    back = weight * back
    gate_grad = (back * up_act * sigma * (1.0 + gate_act * (1.0 - sigma))).astype(jnp.bfloat16)
    up_grad = (back * silu_gate).astype(jnp.bfloat16)
    contrib = f32_dot("rh,hd->rd", gate_grad, gate) + f32_dot("rh,hd->rd", up_grad, up)
    return weighted, gate_grad, up_grad, contrib.astype(jnp.bfloat16)


def body(tokens, route_ids, route_probs, cotangent, w_gate_up, w_down):
    turns = lax.axis_size("dp")
    experts = lax.axis_size("expert")
    here = lax.axis_index("expert")
    hid, width = w_down.shape[1:]
    names = jnp.arange(experts, dtype=jnp.int32) ^ here
    prob = jnp.sum(
        jnp.where(route_ids[None] == names[:, None, None], route_probs[None], 0), axis=2
    ).astype(jnp.bfloat16)

    slabs = [(tokens, cotangent, prob)]
    for _ in range(turns - 1):
        slabs.append(tuple(onward(v) for v in slabs[-1]))
    block = jnp.concatenate([w_gate_up.reshape(2 * hid, width), w_down.reshape(hid, width)])
    blocks = all_experts(block)
    gate = jnp.concatenate([b[:hid] for b in blocks])
    up = jnp.concatenate([b[hid : 2 * hid] for b in blocks])
    down = jnp.concatenate([b[2 * hid :] for b in blocks])

    parts = [hidden_terms(x, dy, pr, gate, up, down) for x, dy, pr in slabs]
    acc = parts[1][3]
    for i in range(2, turns + 1):
        acc = onward(acc)
        acc = (acc.astype(jnp.float32) + parts[i % turns][3].astype(jnp.float32)).astype(jnp.bfloat16)

    all_x = jnp.concatenate([s[0] for s in slabs])
    all_dy = jnp.concatenate([s[1] for s in slabs])
    weighted, gate_grad, up_grad = (jnp.concatenate([p[i] for p in parts]) for i in range(3))
    grad_down = f32_dot("rh,rd->hd", weighted, all_dy).astype(jnp.bfloat16)
    grad_gate = f32_dot("rh,rd->hd", gate_grad, all_x).astype(jnp.bfloat16)
    grad_up = f32_dot("rh,rd->hd", up_grad, all_x).astype(jnp.bfloat16)
    terms = []
    for k in range(experts):
        at = slice(k * hid, (k + 1) * hid)
        terms.append(jnp.concatenate([grad_gate[at], grad_up[at], grad_down[at]]))
    total = summed_to_owner(terms)
    return (
        acc,
        total[: 2 * hid].reshape(1, 2, hid, width),
        total[2 * hid :].reshape(1, hid, width),
    )


def solution(mesh):
    placed = (
        P(("groups", "expert", "dp"), None),
        P(("groups", "expert", "dp"), None),
        P(("groups", "expert", "dp"), None),
        P(("groups", "expert", "dp"), None),
        P("expert", None, "dp", None),
        P("expert", "dp", None),
    )
    return jax.shard_map(
        body,
        mesh=mesh,
        in_specs=placed,
        out_specs=(
            P(("groups", "expert", "dp"), None),
            P(("groups", "expert"), None, "dp", None),
            P(("groups", "expert"), "dp", None),
        ),
        check_vma=False,
    )
```

```python
import functools

import jax
import jax.numpy as jnp
from jax import lax
from jax.experimental import pallas as pl
from jax.experimental.pallas import tpu as pltpu
from jax.sharding import PartitionSpec as P

BF16 = jnp.bfloat16
F32 = jnp.float32


def ring_pairs(count, turns):
    order = [0] + list(range(1, count, 2)) + list(range(2, count, 2))[::-1]
    return [(order[i], order[(i + turns) % count]) for i in range(count)]


def onward(block, turns=1):
    return lax.ppermute(block, "dp", ring_pairs(lax.axis_size("dp"), turns))


def swapped(block, bit):
    return lax.ppermute(block, "expert", [(i, i ^ bit) for i in range(lax.axis_size("expert"))])


def bits_of(count):
    return [1 << i for i in range(count.bit_length() - 1)]


def all_experts(block):
    held = {0: block}
    for bit in bits_of(lax.axis_size("expert"))[::-1]:
        held.update({k | bit: swapped(v, bit) for k, v in list(held.items())})
    return [held[k] for k in range(len(held))]


def summed_to_owner(terms):
    left, sent = dict(enumerate(terms)), None
    for bit in bits_of(len(terms)):
        stay = [k for k in left if not k & bit]
        got = {k: swapped(left[k | bit], bit) for k in stay[::-1]}
        left = {k: left[k].astype(F32) + got[k].astype(F32) for k in stay}
        if len(left) > 1:
            left = {k: v.astype(BF16) for k, v in left.items()}
            sent = left[max(left)]
    return left[0], sent


def call(kernel, outs, *args, flops=0, scratch=()):
    total = sum(a.size * a.dtype.itemsize for a in (*args, *outs))
    return pl.pallas_call(
        kernel,
        out_shape=list(outs),
        in_specs=[pl.BlockSpec(memory_space=pltpu.VMEM)] * len(args),
        out_specs=[pl.BlockSpec(memory_space=pltpu.VMEM)] * len(outs),
        scratch_shapes=list(scratch),
        compiler_params=pltpu.CompilerParams(vmem_limit_bytes=40 * 1024 * 1024),
        cost_estimate=pl.CostEstimate(flops=flops, bytes_accessed=total, transcendentals=0),
    )(*args)


def dot_nt(a, b):
    return lax.dot_general(a, b, (((1,), (1,)), ((), ())), preferred_element_type=F32)


def dot_tn(a, b):
    return lax.dot_general(a, b, (((0,), (0,)), ((), ())), preferred_element_type=F32)


def dot_nn(a, b):
    return jnp.dot(a, b, preferred_element_type=F32)


def grads_of(gate_act, up_act, back, weight):
    sigma = jax.nn.sigmoid(gate_act)
    silu_gate = gate_act * sigma
    weighted = weight * silu_gate * up_act
    back = weight * back
    gate_grad = back * up_act * sigma * (1.0 + gate_act * (1.0 - sigma))
    return gate_grad.astype(BF16), (back * silu_gate).astype(BF16), weighted.astype(BF16)


def spread(refs, *counts):
    at, groups = 0, []
    for count in counts:
        groups.append(refs[at : at + count])
        at += count
    return *groups, refs[at:]


def put_contrib(both, gate_up, contrib):
    wide2, width = gate_up[0].shape
    step = min(512, width)
    for at in range(0, width, step):
        cols = slice(at, at + step)
        total = None
        for k, block in enumerate(gate_up):
            term = dot_tn(both[k * wide2 : (k + 1) * wide2, :], block[:, cols])
            total = term if total is None else total + term
        contrib[:, cols] = total.astype(BF16)


def put_weight_grads(ks, xs, dys, both, hid, gate_up, down):
    wide, width = down[0].shape
    count = xs[0].shape[0]
    step = min(512, width)
    for n, k in enumerate(ks):
        for acts, rows, out, size in ((hid, dys, down[n], wide), (both, xs, gate_up[n], 2 * wide)):
            left = jnp.concatenate([a[k * size : (k + 1) * size, :] for a in acts], axis=1)
            for at in range(0, width, step):
                cols = slice(at, at + step)
                right = jnp.concatenate([r[:count, cols] for r in rows], axis=0)
                out[:, cols] = dot_nn(left, right).astype(BF16)


def weights_of(dyp, experts, rows):
    width = dyp.shape[1]
    per = width // rows
    packed = dyp[rows:, :].astype(F32)
    return [
        packed[k // per : k // per + 1, k % per * rows : (k % per + 1) * rows] for k in range(experts)
    ]


def slab_kernel(experts, *refs):
    (x, dyp), gate_up, down, (both, hid, contrib) = spread(refs, 2, experts, experts)
    rows, wide = x.shape[0], down[0].shape[0]
    weights = weights_of(dyp, experts, rows)
    for k in range(experts):
        acts = dot_nt(gate_up[k][...], x[...])
        back = dot_nt(down[k][...], dyp[:rows, :])
        gate_grad, up_grad, weighted = grads_of(acts[:wide], acts[wide:], back, weights[k])
        both[2 * k * wide : (2 * k + 1) * wide, :] = gate_grad
        both[(2 * k + 1) * wide : (2 * k + 2) * wide, :] = up_grad
        hid[k * wide : (k + 1) * wide, :] = weighted
    put_contrib(both, gate_up, contrib)


def acts_kernel(experts, *refs):
    (x,), gate_up, (acts,) = spread(refs, 1, experts)
    wide = gate_up[0].shape[0] // 2
    for k in range(experts):
        acts[2 * k * wide : 2 * (k + 1) * wide, :] = dot_nt(gate_up[k][...], x[...])


def far_kernel(experts, slabs, ks, *refs):
    (acts,), down, xs, dys, both, hid, outs = spread(
        refs, 1, experts, slabs, slabs, slabs - 1, slabs - 1
    )
    (last, last_hid), out_gate_up, out_down, _ = spread(outs, 2, len(ks), len(ks))
    rows, wide = xs[0].shape[0], down[0].shape[0]
    weights = weights_of(dys[-1], experts, rows)
    for k in range(experts):
        back = dot_nt(down[k][...], dys[-1][:rows, :])
        gate_act = acts[2 * k * wide : (2 * k + 1) * wide, :]
        up_act = acts[(2 * k + 1) * wide : (2 * k + 2) * wide, :]
        gate_grad, up_grad, weighted = grads_of(gate_act, up_act, back, weights[k])
        last[2 * k * wide : (2 * k + 1) * wide, :] = gate_grad
        last[(2 * k + 1) * wide : (2 * k + 2) * wide, :] = up_grad
        last_hid[k * wide : (k + 1) * wide, :] = weighted
    put_weight_grads(ks, xs, dys, (*both, last), (*hid, last_hid), out_gate_up, out_down)


def near_kernel(experts, slabs, ks, *refs):
    gate_up, xs, dys, both, hid, outs = spread(refs, experts, slabs, slabs, slabs, slabs)
    (contrib,), out_gate_up, out_down, _ = spread(outs, 1, len(ks), len(ks))
    put_weight_grads(ks, xs, dys, both, hid, out_gate_up, out_down)
    put_contrib(both[-1], gate_up, contrib)


def shape(rows, cols, kind=BF16):
    return jax.ShapeDtypeStruct((rows, cols), kind)


def after(value, *others):
    return lax.optimization_barrier((value, *others))[0]


def body(tokens, route_ids, route_probs, cotangent, w_gate_up, w_down):
    turns = lax.axis_size("dp")
    experts = lax.axis_size("expert")
    here = lax.axis_index("expert")
    wide, width = w_down.shape[1:]
    names = jnp.arange(experts, dtype=jnp.int32) ^ here

    rows = tokens.shape[0]
    prob = jnp.sum(
        jnp.where(route_ids[None] == names[:, None, None], route_probs[None], 0), axis=2
    ).astype(BF16)
    packed = jnp.zeros((-(-prob.size // (8 * width)) * 8 * width,), BF16).at[: prob.size].set(prob.reshape(-1))
    xs, dys = [tokens], [jnp.concatenate([cotangent, packed.reshape(-1, width)])]
    for _ in range(turns - 1):
        xs.append(onward(xs[-1]))
        dys.append(onward(dys[-1]))
    gate_up = all_experts(w_gate_up.reshape(2 * wide, width))
    down = all_experts(w_down.reshape(wide, width))

    slabs, units = len(xs), experts * wide
    unit_flops = 2 * rows * width * units
    both, hid, contrib = [], [], []
    for x, dyp in zip(xs[:-1], dys):
        b, h, c = call(
            functools.partial(slab_kernel, experts),
            (shape(2 * units, rows), shape(units, rows), shape(rows, width)),
            x, dyp, *gate_up, *down,
            flops=5 * unit_flops,
        )
        both.append(b)
        hid.append(h)
        contrib.append(c)
    (acts,) = call(
        functools.partial(acts_kernel, experts),
        (shape(2 * units, rows, F32),),
        xs[-1], *gate_up,
        flops=2 * unit_flops,
    )

    far = tuple(range(experts // 2, experts))[::-1]
    near = tuple(range(experts // 2))[::-1]
    grads = [shape(2 * wide, width)] * len(far) + [shape(wide, width)] * len(far)
    b, h, *got_far = call(
        functools.partial(far_kernel, experts, slabs, far),
        (shape(2 * units, rows), shape(units, rows), *grads),
        acts, *down, *xs, *dys, *both, *hid,
        flops=3 * slabs * unit_flops // 2 + unit_flops,
    )
    both.append(b)
    hid.append(h)
    c, *got_near = call(
        functools.partial(near_kernel, experts, slabs, near),
        (shape(rows, width), *grads),
        *gate_up, *xs, *dys, *both, *hid,
        flops=3 * slabs * unit_flops // 2 + 2 * unit_flops,
    )
    contrib.append(c)
    terms_gate_up = dict(zip(far + near, got_far[: len(far)] + got_near[: len(near)]))
    terms_down = dict(zip(far + near, got_far[len(far) :] + got_near[len(near) :]))
    grad_down, sent_down = summed_to_owner([terms_down[k] for k in range(experts)])
    grad_gate_up, sent_gate_up = summed_to_owner([terms_gate_up[k] for k in range(experts)])

    half = width // 2
    done = []
    for cols in (slice(0, half), slice(half, width)):
        part = onward(after(contrib[1 % slabs][:, cols], xs[-1]))
        part = after(part, sent_gate_up, sent_down)
        for i in range(2, slabs + 1):
            if i > 2:
                part = onward(part)
            part = (part.astype(F32) + contrib[i % slabs][:, cols].astype(F32)).astype(BF16)
        done.append(part)
    acc = jnp.concatenate(done, axis=1)
    return acc, grad_gate_up.reshape(1, 2, wide, width), grad_down.reshape(1, wide, width)


def solution(mesh):
    placed = (
        P(("groups", "expert", "dp"), None),
        P(("groups", "expert", "dp"), None),
        P(("groups", "expert", "dp"), None),
        P(("groups", "expert", "dp"), None),
        P("expert", None, "dp", None),
        P("expert", "dp", None),
    )
    return jax.shard_map(
        body,
        mesh=mesh,
        in_specs=placed,
        out_specs=(
            P(("groups", "expert", "dp"), None),
            P(("groups", "expert"), None, "dp", None),
            P(("groups", "expert"), "dp", None),
        ),
        check_vma=False,
    )
```

```python
import functools
import math

import jax
import jax.numpy as jnp
from jax import lax
from jax.experimental import pallas as pl
from jax.experimental.pallas import tpu as pltpu
from jax.sharding import PartitionSpec as P

BF16 = jnp.bfloat16
F32 = jnp.float32


def ring_pairs(count, turns):
    order = [0] + list(range(1, count, 2)) + list(range(2, count, 2))[::-1]
    return [(order[i], order[(i + turns) % count]) for i in range(count)]


def onward(block, turns=1):
    return lax.ppermute(block, "dp", ring_pairs(lax.axis_size("dp"), turns))


def swapped(block, bit):
    return lax.ppermute(block, "expert", [(i, i ^ bit) for i in range(lax.axis_size("expert"))])


def bits_of(count):
    return [1 << i for i in range(count.bit_length() - 1)]


def all_experts(block):
    held = {0: block}
    for bit in bits_of(lax.axis_size("expert"))[::-1]:
        held.update({k | bit: swapped(v, bit) for k, v in list(held.items())})
    return [held[k] for k in range(len(held))]


def call(kernel, outs, *args, flops=0, scratch=()):
    total = sum(a.size * a.dtype.itemsize for a in (*args, *outs))
    return pl.pallas_call(
        kernel,
        out_shape=list(outs),
        in_specs=[pl.BlockSpec(memory_space=pltpu.VMEM)] * len(args),
        out_specs=[pl.BlockSpec(memory_space=pltpu.VMEM)] * len(outs),
        scratch_shapes=list(scratch),
        compiler_params=pltpu.CompilerParams(vmem_limit_bytes=40 * 1024 * 1024),
        cost_estimate=pl.CostEstimate(flops=flops, bytes_accessed=total, transcendentals=0),
    )(*args)


def dot_nt(a, b):
    return lax.dot_general(a, b, (((1,), (1,)), ((), ())), preferred_element_type=F32)


def dot_tn(a, b):
    return lax.dot_general(a, b, (((0,), (0,)), ((), ())), preferred_element_type=F32)


def dot_nn(a, b):
    return jnp.dot(a, b, preferred_element_type=F32)


def grads_of(gate_act, up_act, back, weight):
    sigma = jax.nn.sigmoid(gate_act)
    silu_gate = gate_act * sigma
    weighted = weight * silu_gate * up_act
    back = weight * back
    gate_grad = back * up_act * sigma * (1.0 + gate_act * (1.0 - sigma))
    return gate_grad.astype(BF16), (back * silu_gate).astype(BF16), weighted.astype(BF16)


def spread(refs, *counts):
    at, groups = 0, []
    for count in counts:
        groups.append(refs[at : at + count])
        at += count
    return *groups, refs[at:]


def put_contrib(both, gate_up, contrib):
    wide2, width = gate_up[0].shape
    step = min(512, width)
    for at in range(0, width, step):
        cols = slice(at, at + step)
        total = None
        for k, block in enumerate(gate_up):
            term = dot_tn(both[k * wide2 : (k + 1) * wide2, :], block[:, cols])
            total = term if total is None else total + term
        contrib[:, cols] = total.astype(BF16)


def put_weight_grads(ks, split, xs, dys, both, hid, outs):
    rows, width = xs[0].shape
    block = dys[0].shape[1]
    for k in ks:
        mine, outs = (outs[:3], outs[3:]) if k in split else (outs[:1], outs[1:])
        wide = sum(o.shape[0] for o in mine) // 3
        left_x = jnp.concatenate([a[2 * k * wide : 2 * (k + 1) * wide, :] for a in both], axis=1)
        left_dy = jnp.concatenate([a[k * wide : (k + 1) * wide, :] for a in hid], axis=1)
        for n in range(width // block):
            cols = slice(n * block, (n + 1) * block)
            right_x = jnp.concatenate([x[:, cols] for x in xs], axis=0)
            right_dy = jnp.concatenate([dy[n * rows : (n + 1) * rows, :] for dy in dys], axis=0)
            got_x = dot_nn(left_x, right_x).astype(BF16)
            got_dy = dot_nn(left_dy, right_dy).astype(BF16)
            if len(mine) == 1:
                mine[0][: 2 * wide, cols] = got_x
                mine[0][2 * wide :, cols] = got_dy
            else:
                mine[0][:, cols] = got_x[:wide]
                mine[1][:, cols] = got_x[wide:]
                mine[2][:, cols] = got_dy


def sum_kernel(counts, *refs):
    parts, outs = [], refs[sum(counts) :]
    for count in counts:
        parts.append(refs[:count])
        refs = refs[count:]
    size = math.gcd(*(r.shape[0] for part in (*parts, outs) for r in part))

    def rows_at(part, at):
        for ref in part:
            if at < ref.shape[0]:
                return ref, slice(at, at + size)
            at -= ref.shape[0]

    for at in range(0, sum(r.shape[0] for r in outs), size):
        total = None
        for part in parts:
            ref, rows = rows_at(part, at)
            term = ref[rows, :].astype(F32)
            total = term if total is None else total + term
        ref, rows = rows_at(outs, at)
        ref[rows, :] = total.astype(ref.dtype)


def summed(addends, outs):
    counts = tuple(len(a) for a in addends)
    return call(functools.partial(sum_kernel, counts), outs, *(r for a in addends for r in a))


def travelling(dy, prob):
    rows, width = dy.shape
    block = 2 * rows if width % (2 * rows) == 0 else width
    stacked = dy.reshape(rows, width // block, block).transpose(1, 0, 2).reshape(-1, block)
    below = -(-prob.size // (16 * block)) * 16
    packed = jnp.zeros((below * block,), BF16).at[: prob.size].set(prob.reshape(-1))
    return jnp.concatenate([stacked, packed.reshape(below, block)])


def weights_of(dyp, experts, rows, width):
    block = dyp.shape[1]
    per = block // rows
    packed = dyp[width // block * rows :, :].astype(F32)
    return [
        packed[k // per : k // per + 1, k % per * rows : (k % per + 1) * rows] for k in range(experts)
    ]


def back_of(down, dyp, rows):
    block = dyp.shape[1]
    total = None
    for n in range(down.shape[1] // block):
        term = dot_nt(down[:, n * block : (n + 1) * block], dyp[n * rows : (n + 1) * rows, :])
        total = term if total is None else total + term
    return total


def slab_kernel(experts, *refs):
    (x, dyp), gate_up, down, (both, hid, contrib) = spread(refs, 2, experts, experts)
    rows, wide = x.shape[0], down[0].shape[0]
    weights = weights_of(dyp, experts, rows, x.shape[1])
    for k in range(experts):
        acts = dot_nt(gate_up[k][...], x[...])
        back = back_of(down[k], dyp, rows)
        gate_grad, up_grad, weighted = grads_of(acts[:wide], acts[wide:], back, weights[k])
        both[2 * k * wide : (2 * k + 1) * wide, :] = gate_grad
        both[(2 * k + 1) * wide : (2 * k + 2) * wide, :] = up_grad
        hid[k * wide : (k + 1) * wide, :] = weighted
    put_contrib(both, gate_up, contrib)


def acts_kernel(experts, *refs):
    (x,), gate_up, (acts,) = spread(refs, 1, experts)
    wide = gate_up[0].shape[0] // 2
    for k in range(experts):
        acts[2 * k * wide : 2 * (k + 1) * wide, :] = dot_nt(gate_up[k][...], x[...])


def far_kernel(experts, slabs, ks, split, *refs):
    (acts,), down, xs, dys, both, hid, outs = spread(
        refs, 1, experts, slabs, slabs, slabs - 1, slabs - 1
    )
    (last, last_hid), grads = spread(outs, 2)
    rows, wide = xs[0].shape[0], down[0].shape[0]
    weights = weights_of(dys[-1], experts, rows, down[0].shape[1])
    for k in range(experts):
        back = back_of(down[k], dys[-1], rows)
        gate_act = acts[2 * k * wide : (2 * k + 1) * wide, :]
        up_act = acts[(2 * k + 1) * wide : (2 * k + 2) * wide, :]
        gate_grad, up_grad, weighted = grads_of(gate_act, up_act, back, weights[k])
        last[2 * k * wide : (2 * k + 1) * wide, :] = gate_grad
        last[(2 * k + 1) * wide : (2 * k + 2) * wide, :] = up_grad
        last_hid[k * wide : (k + 1) * wide, :] = weighted
    put_weight_grads(ks, split, xs, dys, (*both, last), (*hid, last_hid), grads)


def near_kernel(experts, slabs, ks, *refs):
    gate_up, xs, dys, both, hid, outs = spread(refs, experts, slabs, slabs, slabs, slabs)
    (contrib,), grads = spread(outs, 1)
    put_weight_grads(ks, (), xs, dys, both, hid, grads)
    put_contrib(both[-1], gate_up, contrib)


def shape(rows, cols, kind=BF16):
    return jax.ShapeDtypeStruct((rows, cols), kind)


def after(value, *others):
    return lax.optimization_barrier((value, *others))[0]


def body(tokens, route_ids, route_probs, cotangent, w_gate_up, w_down):
    turns = lax.axis_size("dp")
    experts = lax.axis_size("expert")
    here = lax.axis_index("expert")
    wide, width = w_down.shape[1:]
    names = jnp.arange(experts, dtype=jnp.int32) ^ here

    rows = tokens.shape[0]
    prob = jnp.sum(
        jnp.where(route_ids[None] == names[:, None, None], route_probs[None], 0), axis=2
    ).astype(BF16)
    xs, dys = [tokens], [travelling(cotangent, prob)]
    for _ in range(turns - 1):
        xs.append(onward(xs[-1]))
        dys.append(onward(dys[-1]))
    gate_up = all_experts(after(w_gate_up, prob).reshape(2 * wide, width))
    down = all_experts(w_down.reshape(wide, width))

    slabs, units = len(xs), experts * wide
    unit_flops = 2 * rows * width * units
    both, hid, contrib = [], [], []
    for x, dyp in zip(xs[:-1], dys):
        b, h, c = call(
            functools.partial(slab_kernel, experts),
            (shape(2 * units, rows), shape(units, rows), shape(rows, width)),
            x, dyp, *gate_up, *down,
            flops=5 * unit_flops,
        )
        both.append(b)
        hid.append(h)
        contrib.append(c)
    (acts,) = call(
        functools.partial(acts_kernel, experts),
        (shape(2 * units, rows, F32),),
        xs[-1], *gate_up,
        flops=2 * unit_flops,
    )

    far = tuple(range(experts // 2, experts))[::-1]
    near = tuple(range(experts // 2))[::-1]
    split = tuple(k for k in far if k % 2)
    whole, third = shape(3 * wide, width), shape(wide, width)
    grads = [piece for k in far for piece in ([third] * 3 if k in split else [whole])]
    b, h, *got_far = call(
        functools.partial(far_kernel, experts, slabs, far, split),
        (shape(2 * units, rows), shape(units, rows), *grads),
        acts, *down, *xs, *dys, *both, *hid,
        flops=3 * slabs * unit_flops // 2 + unit_flops,
    )
    both.append(b)
    hid.append(h)
    c, *got_near = call(
        functools.partial(near_kernel, experts, slabs, near),
        (shape(rows, width), *[whole] * len(near)),
        *gate_up, *xs, *dys, *both, *hid,
        flops=3 * slabs * unit_flops // 2 + 2 * unit_flops,
    )
    contrib.append(c)
    terms = {k: [(got,)] for k, got in zip(near, got_near)}
    for k in far:
        count = 3 if k in split else 1
        terms[k], got_far = [tuple(got_far[:count])], got_far[count:]

    total = contrib[0].astype(F32)
    if slabs > 1:
        total = total + onward(after(contrib[1], both[-1]), -1).astype(F32)
    acc = None
    if slabs > 2:
        acc = onward(after(contrib[2], acts, *both[:-1]))
    for bit in bits_of(experts):
        for k in sorted((k for k in terms if k & bit), reverse=True):
            out = terms.pop(k)
            if len(out) > 1:
                out = [summed(out, [whole])]
                if bit == 2 and acc is not None:
                    acc = after(acc, *out[0])
            terms[k ^ bit].append(tuple(swapped(v, bit) for v in out[0]))
    grad_gate_up, grad_down = summed(terms[0], [shape(2 * wide, width, F32), shape(wide, width, F32)])

    for i in range(3, slabs):
        acc = onward((acc.astype(F32) + contrib[i].astype(F32)).astype(BF16))
    if slabs > 2:
        total = total + acc.astype(F32)
    acc = total.astype(BF16)
    return acc, grad_gate_up.reshape(1, 2, wide, width), grad_down.reshape(1, wide, width)


def solution(mesh):
    placed = (
        P(("groups", "expert", "dp"), None),
        P(("groups", "expert", "dp"), None),
        P(("groups", "expert", "dp"), None),
        P(("groups", "expert", "dp"), None),
        P("expert", None, "dp", None),
        P("expert", "dp", None),
    )
    return jax.shard_map(
        body,
        mesh=mesh,
        in_specs=placed,
        out_specs=(
            P(("groups", "expert", "dp"), None),
            P(("groups", "expert"), None, "dp", None),
            P(("groups", "expert"), "dp", None),
        ),
        check_vma=False,
    )
```

```python
import functools
import math

import jax
import jax.numpy as jnp
from jax import lax
from jax.experimental import pallas as pl
from jax.experimental.pallas import tpu as pltpu
from jax.sharding import PartitionSpec as P

BF16 = jnp.bfloat16
COSTS = {"slab": 2, "acts": 4, "far": 1, "even": 5, "near": 2, "join": 1, "tokens": 4, "last": 2}
F32 = jnp.float32


def ring_pairs(count, turns):
    order = [0] + list(range(1, count, 2)) + list(range(2, count, 2))[::-1]
    return [(order[i], order[(i + turns) % count]) for i in range(count)]


def onward(block, turns=1):
    return lax.ppermute(block, "dp", ring_pairs(lax.axis_size("dp"), turns))


def swapped(block, bit):
    return lax.ppermute(block, "expert", [(i, i ^ bit) for i in range(lax.axis_size("expert"))])


def bits_of(count):
    return [1 << i for i in range(count.bit_length() - 1)]


def all_experts(block):
    held = {0: block}
    for bit in bits_of(lax.axis_size("expert"))[::-1]:
        held.update({k | bit: swapped(v, bit) for k, v in list(held.items())})
    return [held[k] for k in range(len(held))]


def call(kernel, outs, *args, cost=0.0, scratch=()):
    return pl.pallas_call(
        kernel,
        out_shape=list(outs),
        in_specs=[pl.BlockSpec(memory_space=pltpu.VMEM)] * len(args),
        out_specs=[pl.BlockSpec(memory_space=pltpu.VMEM)] * len(outs),
        scratch_shapes=list(scratch),
        compiler_params=pltpu.CompilerParams(vmem_limit_bytes=40 * 1024 * 1024),
        cost_estimate=pl.CostEstimate(flops=int(cost * 1e9), bytes_accessed=0, transcendentals=0),
    )(*args)


def dot_nt(a, b):
    return lax.dot_general(a, b, (((1,), (1,)), ((), ())), preferred_element_type=F32)


def dot_tn(a, b):
    return lax.dot_general(a, b, (((0,), (0,)), ((), ())), preferred_element_type=F32)


def dot_nn(a, b):
    return jnp.dot(a, b, preferred_element_type=F32)


def grads_of(gate_act, up_act, back, weight):
    sigma = jax.nn.sigmoid(gate_act)
    silu_gate = gate_act * sigma
    weighted = weight * silu_gate * up_act
    back = weight * back
    gate_grad = back * up_act * sigma * (1.0 + gate_act * (1.0 - sigma))
    return gate_grad.astype(BF16), (back * silu_gate).astype(BF16), weighted.astype(BF16)


def spread(refs, *counts):
    at, groups = 0, []
    for count in counts:
        groups.append(refs[at : at + count])
        at += count
    return *groups, refs[at:]


def put_contrib(both, gate_up, contrib):
    wide2, width = gate_up[0].shape
    step = min(512, width)
    for at in range(0, width, step):
        cols = slice(at, at + step)
        total = None
        for k, block in enumerate(gate_up):
            term = dot_tn(both[k * wide2 : (k + 1) * wide2, :], block[:, cols])
            total = term if total is None else total + term
        contrib[:, cols] = total.astype(BF16)


def put_weight_grads(ks, split, xs, dys, both, hid, outs):
    rows, width = xs[0].shape
    block = dys[0].shape[1]
    for k in ks:
        mine, outs = (outs[:3], outs[3:]) if k in split else (outs[:1], outs[1:])
        wide = sum(o.shape[0] for o in mine) // 3
        left_x = jnp.concatenate([a[2 * k * wide : 2 * (k + 1) * wide, :] for a in both], axis=1)
        left_dy = jnp.concatenate([a[k * wide : (k + 1) * wide, :] for a in hid], axis=1)
        for n in range(width // block):
            cols = slice(n * block, (n + 1) * block)
            right_x = jnp.concatenate([x[:, cols] for x in xs], axis=0)
            right_dy = jnp.concatenate([dy[n * rows : (n + 1) * rows, :] for dy in dys], axis=0)
            got_x = dot_nn(left_x, right_x).astype(BF16)
            got_dy = dot_nn(left_dy, right_dy).astype(BF16)
            if len(mine) == 1:
                mine[0][: 2 * wide, cols] = got_x
                mine[0][2 * wide :, cols] = got_dy
            else:
                mine[0][:, cols] = got_x[:wide]
                mine[1][:, cols] = got_x[wide:]
                mine[2][:, cols] = got_dy


def sum_kernel(counts, *refs):
    parts, outs = [], refs[sum(counts) :]
    for count in counts:
        parts.append(refs[:count])
        refs = refs[count:]
    size = math.gcd(*(r.shape[0] for part in (*parts, outs) for r in part))

    def rows_at(part, at):
        for ref in part:
            if at < ref.shape[0]:
                return ref, slice(at, at + size)
            at -= ref.shape[0]

    for at in range(0, sum(r.shape[0] for r in outs), size):
        total = None
        for part in parts:
            ref, rows = rows_at(part, at)
            term = ref[rows, :].astype(F32)
            total = term if total is None else total + term
        ref, rows = rows_at(outs, at)
        ref[rows, :] = total.astype(ref.dtype)


def finish_kernel(count, *refs):
    terms, refs = refs[:count], refs[count:]
    outs, held, sems = refs[: len(refs) // 2], refs[len(refs) // 2 : -1], refs[-1]
    copies, first = [], 0
    for out, buffer in zip(outs, held):
        rows = out.shape[0] // 2
        for at in (0, rows):
            total = None
            for ref in terms:
                term = ref[first : first + rows, :].astype(F32)
                total = term if total is None else total + term
            buffer[at : at + rows, :] = total.astype(buffer.dtype)
            copy = pltpu.make_async_copy(
                buffer.at[at : at + rows, :], out.at[at : at + rows, :], sems.at[len(copies)]
            )
            copy.start()
            copies.append(copy)
            first += rows
    for copy in copies:
        copy.wait()


def finished(args, outs, cost):
    return pl.pallas_call(
        functools.partial(finish_kernel, len(args)),
        out_shape=list(outs),
        in_specs=[pl.BlockSpec(memory_space=pltpu.VMEM)] * len(args),
        out_specs=[pl.BlockSpec(memory_space=pl.ANY)] * len(outs),
        scratch_shapes=[
            *[pltpu.VMEM(o.shape, o.dtype) for o in outs],
            pltpu.SemaphoreType.DMA((2 * len(outs),)),
        ],
        compiler_params=pltpu.CompilerParams(vmem_limit_bytes=40 * 1024 * 1024),
        cost_estimate=pl.CostEstimate(flops=int(cost * 1e9), bytes_accessed=0, transcendentals=0),
    )(*args)


def summed(addends, outs, cost=0.0):
    counts = tuple(len(a) for a in addends)
    return call(functools.partial(sum_kernel, counts), outs, *(r for a in addends for r in a), cost=cost)


def travelling(dy, prob):
    rows, width = dy.shape
    block = 2 * rows if width % (2 * rows) == 0 else width
    stacked = dy.reshape(rows, width // block, block).transpose(1, 0, 2).reshape(-1, block)
    below = -(-prob.size // (16 * block)) * 16
    packed = jnp.zeros((below * block,), BF16).at[: prob.size].set(prob.reshape(-1))
    return jnp.concatenate([stacked, packed.reshape(below, block)])


def weights_of(dyp, experts, rows, width):
    block = dyp.shape[1]
    per = block // rows
    packed = dyp[width // block * rows :, :].astype(F32)
    return [
        packed[k // per : k // per + 1, k % per * rows : (k % per + 1) * rows] for k in range(experts)
    ]


def back_of(down, dyp, rows):
    block = dyp.shape[1]
    total = None
    for n in range(down.shape[1] // block):
        term = dot_nt(down[:, n * block : (n + 1) * block], dyp[n * rows : (n + 1) * rows, :])
        total = term if total is None else total + term
    return total


def slab_kernel(experts, *refs):
    (x, dyp), gate_up, down, (both, hid, contrib) = spread(refs, 2, experts, experts)
    rows, wide = x.shape[0], down[0].shape[0]
    weights = weights_of(dyp, experts, rows, x.shape[1])
    for k in range(experts):
        acts = dot_nt(gate_up[k][...], x[...])
        back = back_of(down[k], dyp, rows)
        gate_grad, up_grad, weighted = grads_of(acts[:wide], acts[wide:], back, weights[k])
        both[2 * k * wide : (2 * k + 1) * wide, :] = gate_grad
        both[(2 * k + 1) * wide : (2 * k + 2) * wide, :] = up_grad
        hid[k * wide : (k + 1) * wide, :] = weighted
    put_contrib(both, gate_up, contrib)


def acts_kernel(experts, *refs):
    (x,), gate_up, (acts,) = spread(refs, 1, experts)
    wide = gate_up[0].shape[0] // 2
    for k in range(experts):
        acts[2 * k * wide : 2 * (k + 1) * wide, :] = dot_nt(gate_up[k][...], x[...])


def far_kernel(experts, slabs, ks, split, *refs):
    (acts,), down, xs, dys, both, hid, outs = spread(
        refs, 1, experts, slabs, slabs, slabs - 1, slabs - 1
    )
    (last, last_hid), grads = spread(outs, 2)
    rows, wide = xs[0].shape[0], down[0].shape[0]
    weights = weights_of(dys[-1], experts, rows, down[0].shape[1])
    for k in range(experts):
        back = back_of(down[k], dys[-1], rows)
        gate_act = acts[2 * k * wide : (2 * k + 1) * wide, :]
        up_act = acts[(2 * k + 1) * wide : (2 * k + 2) * wide, :]
        gate_grad, up_grad, weighted = grads_of(gate_act, up_act, back, weights[k])
        last[2 * k * wide : (2 * k + 1) * wide, :] = gate_grad
        last[(2 * k + 1) * wide : (2 * k + 2) * wide, :] = up_grad
        last_hid[k * wide : (k + 1) * wide, :] = weighted
    put_weight_grads(ks, split, xs, dys, (*both, last), (*hid, last_hid), grads)


def grads_kernel(slabs, ks, *refs):
    xs, dys, both, hid, grads = spread(refs, slabs, slabs, slabs, slabs)
    put_weight_grads(ks, (), xs, dys, both, hid, grads)


def near_kernel(experts, slabs, ks, *refs):
    gate_up, xs, dys, both, hid, outs = spread(refs, experts, slabs, slabs, slabs, slabs)
    (contrib,), grads = spread(outs, 1)
    put_weight_grads(ks, (), xs, dys, both, hid, grads)
    put_contrib(both[-1], gate_up, contrib)


def shape(rows, cols, kind=BF16):
    return jax.ShapeDtypeStruct((rows, cols), kind)


def after(value, *others):
    return lax.optimization_barrier((value, *others))[0] if others else value


def body(tokens, route_ids, route_probs, cotangent, w_gate_up, w_down):
    turns = lax.axis_size("dp")
    experts = lax.axis_size("expert")
    here = lax.axis_index("expert")
    wide, width = w_down.shape[1:]
    names = jnp.arange(experts, dtype=jnp.int32) ^ here

    rows = tokens.shape[0]
    prob = jnp.sum(
        jnp.where(route_ids[None] == names[:, None, None], route_probs[None], 0), axis=2
    ).astype(BF16)
    xs, dys = [tokens], [travelling(cotangent, prob)]
    for _ in range(turns - 1):
        xs.append(onward(xs[-1]))
        dys.append(onward(dys[-1]))
    gate_up = all_experts(after(w_gate_up, prob).reshape(2 * wide, width))
    down = all_experts(w_down.reshape(wide, width))

    slabs, units = len(xs), experts * wide
    both, hid, contrib = [], [], []
    for x, dyp in zip(xs[:-1], dys):
        b, h, c = call(
            functools.partial(slab_kernel, experts),
            (shape(2 * units, rows), shape(units, rows), shape(rows, width)),
            x, dyp, *gate_up, *down,
            cost=COSTS["slab"],
        )
        both.append(b)
        hid.append(h)
        contrib.append(c)
    (acts,) = call(
        functools.partial(acts_kernel, experts),
        (shape(2 * units, rows, F32),),
        xs[-1], *gate_up,
        cost=COSTS["acts"],
    )

    far = tuple(range(experts // 2, experts))[::-1]
    near = tuple(range(experts // 2))[::-1]
    split = tuple(k for k in far if k % 2)
    even = tuple(k for k in far if not k % 2)
    whole, third = shape(3 * wide, width), shape(wide, width)
    b, h, *got_split = call(
        functools.partial(far_kernel, experts, slabs, split, split),
        (shape(2 * units, rows), shape(units, rows), *[third] * (3 * len(split))),
        acts, *down, *xs, *dys, *both, *hid,
        cost=COSTS["far"],
    )
    both.append(b)
    hid.append(h)
    got_even = call(
        functools.partial(grads_kernel, slabs, even),
        [whole] * len(even),
        *xs, *dys, *both, *hid,
        cost=COSTS["even"],
    )
    got_far = []
    for k in far:
        if k in split:
            got_far, got_split = [*got_far, *got_split[:3]], got_split[3:]
        else:
            got_far, got_even = [*got_far, got_even[0]], got_even[1:]
    terms = {}
    for k in far:
        count = 3 if k in split else 1
        terms[k], got_far = [tuple(got_far[:count])], got_far[count:]
    first_bit, *other_bits = bits_of(experts)

    def swap_out(ks, bit):
        for k in ks:
            out = terms.pop(k)
            if len(out) > 1:
                out = [summed(out, [whole])]
                joined.extend(out[0])
            terms.setdefault(k ^ bit, []).append(tuple(swapped(v, bit) for v in out[0]))

    joined = []
    swap_out(split, first_bit)
    if len(other_bits) == 1:
        out = summed(terms.pop(even[0]), [whole], COSTS["join"])
        joined.extend(out)
        terms[0] = [(swapped(out[0], other_bits[0]),)]
    c, *got_near = call(
        functools.partial(near_kernel, experts, slabs, near),
        (shape(rows, width), *[whole] * len(near)),
        *gate_up, *xs, *dys, *both[:-1], after(both[-1], *joined), *hid,
        cost=COSTS["near"],
    )
    contrib.append(c)
    for k, got in zip(near, got_near):
        terms.setdefault(k, []).insert(0, (got,))
    back = [onward(after(contrib[1], *joined), -1)] if slabs > 1 else []
    acc = None
    if slabs > 2:
        acc = onward(after(contrib[2], acts))
    if acc is not None and joined:
        acc = after(acc, *joined)
    swap_out([k for k in near if k % 2], first_bit)
    if len(other_bits) != 1:
        for bit in other_bits:
            swap_out(sorted((k for k in terms if k & bit), reverse=True), bit)
    for i in range(3, slabs):
        acc = onward((acc.astype(F32) + contrib[i].astype(F32)).astype(BF16))
    tokens_terms = [contrib[0], *back, *([acc] if slabs > 2 else [])]
    (acc,) = finished(tokens_terms, [shape(rows, width)], COSTS["tokens"])
    own, *others = [t for (t,) in terms[0]]
    grad_gate_up, grad_down = finished(
        [after(own, acc), *others], [shape(2 * wide, width, F32), shape(wide, width, F32)], COSTS["last"]
    )
    return acc, grad_gate_up.reshape(1, 2, wide, width), grad_down.reshape(1, wide, width)


def solution(mesh):
    placed = (
        P(("groups", "expert", "dp"), None),
        P(("groups", "expert", "dp"), None),
        P(("groups", "expert", "dp"), None),
        P(("groups", "expert", "dp"), None),
        P("expert", None, "dp", None),
        P("expert", "dp", None),
    )
    return jax.shard_map(
        body,
        mesh=mesh,
        in_specs=placed,
        out_specs=(
            P(("groups", "expert", "dp"), None),
            P(("groups", "expert"), None, "dp", None),
            P(("groups", "expert"), "dp", None),
        ),
        check_vma=False,
    )
```

```python
import functools
import math

import jax
import jax.numpy as jnp
from jax import lax
from jax.experimental import pallas as pl
from jax.experimental.pallas import tpu as pltpu
from jax.sharding import PartitionSpec as P

BF16 = jnp.bfloat16
COSTS = {"slab": 2, "acts": 4, "far": 1, "even": 5, "near": 2, "join": 1, "add": 8, "last": 2}
F32 = jnp.float32


def ring_pairs(count, turns):
    order = [0] + list(range(1, count, 2)) + list(range(2, count, 2))[::-1]
    return [(order[i], order[(i + turns) % count]) for i in range(count)]


def onward(block, turns=1):
    return lax.ppermute(block, "dp", ring_pairs(lax.axis_size("dp"), turns))


def swapped(block, bit):
    return lax.ppermute(block, "expert", [(i, i ^ bit) for i in range(lax.axis_size("expert"))])


def bits_of(count):
    return [1 << i for i in range(count.bit_length() - 1)]


def all_experts(block):
    held = {0: block}
    for bit in bits_of(lax.axis_size("expert"))[::-1]:
        held.update({k | bit: swapped(v, bit) for k, v in list(held.items())})
    return [held[k] for k in range(len(held))]


def call(kernel, outs, *args, cost=0.0, scratch=()):
    return pl.pallas_call(
        kernel,
        out_shape=list(outs),
        in_specs=[pl.BlockSpec(memory_space=pltpu.VMEM)] * len(args),
        out_specs=[pl.BlockSpec(memory_space=pltpu.VMEM)] * len(outs),
        scratch_shapes=list(scratch),
        compiler_params=pltpu.CompilerParams(vmem_limit_bytes=40 * 1024 * 1024),
        cost_estimate=pl.CostEstimate(flops=int(cost * 1e9), bytes_accessed=0, transcendentals=0),
    )(*args)


def dot_nt(a, b):
    return lax.dot_general(a, b, (((1,), (1,)), ((), ())), preferred_element_type=F32)


def dot_tn(a, b):
    return lax.dot_general(a, b, (((0,), (0,)), ((), ())), preferred_element_type=F32)


def dot_nn(a, b):
    return jnp.dot(a, b, preferred_element_type=F32)


def grads_of(gate_act, up_act, back, weight):
    sigma = jax.nn.sigmoid(gate_act)
    silu_gate = gate_act * sigma
    weighted = weight * silu_gate * up_act
    back = weight * back
    gate_grad = back * up_act * sigma * (1.0 + gate_act * (1.0 - sigma))
    return gate_grad.astype(BF16), (back * silu_gate).astype(BF16), weighted.astype(BF16)


def spread(refs, *counts):
    at, groups = 0, []
    for count in counts:
        groups.append(refs[at : at + count])
        at += count
    return *groups, refs[at:]


def put_contrib(both, gate_up, contrib):
    wide2, width = gate_up[0].shape
    step = min(512, width)
    for at in range(0, width, step):
        cols = slice(at, at + step)
        total = None
        for k, block in enumerate(gate_up):
            term = dot_tn(both[k * wide2 : (k + 1) * wide2, :], block[:, cols])
            total = term if total is None else total + term
        contrib[:, cols] = total.astype(BF16)


def put_weight_grads(ks, split, xs, dys, both, hid, outs):
    rows, width = xs[0].shape
    block = dys[0].shape[1]
    for k in ks:
        mine, outs = (outs[:3], outs[3:]) if k in split else (outs[:1], outs[1:])
        wide = sum(o.shape[0] for o in mine) // 3
        left_x = jnp.concatenate([a[2 * k * wide : 2 * (k + 1) * wide, :] for a in both], axis=1)
        left_dy = jnp.concatenate([a[k * wide : (k + 1) * wide, :] for a in hid], axis=1)
        for n in range(width // block):
            cols = slice(n * block, (n + 1) * block)
            right_x = jnp.concatenate([x[:, cols] for x in xs], axis=0)
            right_dy = jnp.concatenate([dy[n * rows : (n + 1) * rows, :] for dy in dys], axis=0)
            got_x = dot_nn(left_x, right_x).astype(BF16)
            got_dy = dot_nn(left_dy, right_dy).astype(BF16)
            if len(mine) == 1:
                mine[0][: 2 * wide, cols] = got_x
                mine[0][2 * wide :, cols] = got_dy
            else:
                mine[0][:, cols] = got_x[:wide]
                mine[1][:, cols] = got_x[wide:]
                mine[2][:, cols] = got_dy


def sum_kernel(counts, *refs):
    parts, outs = [], refs[sum(counts) :]
    for count in counts:
        parts.append(refs[:count])
        refs = refs[count:]
    size = math.gcd(*(r.shape[0] for part in (*parts, outs) for r in part))

    def rows_at(part, at):
        for ref in part:
            if at < ref.shape[0]:
                return ref, slice(at, at + size)
            at -= ref.shape[0]

    for at in range(0, sum(r.shape[0] for r in outs), size):
        total = None
        for part in parts:
            ref, rows = rows_at(part, at)
            term = ref[rows, :].astype(F32)
            total = term if total is None else total + term
        ref, rows = rows_at(outs, at)
        ref[rows, :] = total.astype(ref.dtype)


def finish_kernel(counts, *refs):
    groups, refs = [refs[: counts[0]], refs[counts[0] : sum(counts)]], refs[sum(counts) :]
    outs, held, sems = refs[: len(refs) // 2], refs[len(refs) // 2 : -1], refs[-1]
    copies, first = [], [0, 0]
    for n, (out, buffer) in enumerate(zip(outs, held)):
        group = min(n, 1)
        rows = out.shape[0] // 2
        for at in (0, rows):
            total = None
            for ref in groups[group]:
                term = ref[first[group] : first[group] + rows, :].astype(F32)
                total = term if total is None else total + term
            buffer[at : at + rows, :] = total.astype(buffer.dtype)
            copy = pltpu.make_async_copy(
                buffer.at[at : at + rows, :], out.at[at : at + rows, :], sems.at[len(copies)]
            )
            copy.start()
            copies.append(copy)
            first[group] += rows
    for copy in copies:
        copy.wait()


def finished(groups, outs, cost):
    args = [r for group in groups for r in group]
    return pl.pallas_call(
        functools.partial(finish_kernel, tuple(len(g) for g in groups)),
        out_shape=list(outs),
        in_specs=[pl.BlockSpec(memory_space=pltpu.VMEM)] * len(args),
        out_specs=[pl.BlockSpec(memory_space=pl.ANY)] * len(outs),
        scratch_shapes=[
            *[pltpu.VMEM(o.shape, o.dtype) for o in outs],
            pltpu.SemaphoreType.DMA((2 * len(outs),)),
        ],
        compiler_params=pltpu.CompilerParams(vmem_limit_bytes=40 * 1024 * 1024),
        cost_estimate=pl.CostEstimate(flops=int(cost * 1e9), bytes_accessed=0, transcendentals=0),
    )(*args)


def summed(addends, outs, cost=0.0):
    counts = tuple(len(a) for a in addends)
    return call(functools.partial(sum_kernel, counts), outs, *(r for a in addends for r in a), cost=cost)


def travelling(dy, prob):
    rows, width = dy.shape
    block = 2 * rows if width % (2 * rows) == 0 else width
    stacked = dy.reshape(rows, width // block, block).transpose(1, 0, 2).reshape(-1, block)
    below = -(-prob.size // (16 * block)) * 16
    packed = jnp.zeros((below * block,), BF16).at[: prob.size].set(prob.reshape(-1))
    return jnp.concatenate([stacked, packed.reshape(below, block)])


def weights_of(dyp, experts, rows, width):
    block = dyp.shape[1]
    per = block // rows
    packed = dyp[width // block * rows :, :].astype(F32)
    return [
        packed[k // per : k // per + 1, k % per * rows : (k % per + 1) * rows] for k in range(experts)
    ]


def back_of(down, dyp, rows):
    block = dyp.shape[1]
    total = None
    for n in range(down.shape[1] // block):
        term = dot_nt(down[:, n * block : (n + 1) * block], dyp[n * rows : (n + 1) * rows, :])
        total = term if total is None else total + term
    return total


def slab_kernel(experts, *refs):
    (x, dyp), gate_up, down, (both, hid, contrib) = spread(refs, 2, experts, experts)
    rows, wide = x.shape[0], down[0].shape[0]
    weights = weights_of(dyp, experts, rows, x.shape[1])
    for k in range(experts):
        acts = dot_nt(gate_up[k][...], x[...])
        back = back_of(down[k], dyp, rows)
        gate_grad, up_grad, weighted = grads_of(acts[:wide], acts[wide:], back, weights[k])
        both[2 * k * wide : (2 * k + 1) * wide, :] = gate_grad
        both[(2 * k + 1) * wide : (2 * k + 2) * wide, :] = up_grad
        hid[k * wide : (k + 1) * wide, :] = weighted
    put_contrib(both, gate_up, contrib)


def acts_kernel(experts, *refs):
    (x,), gate_up, (acts,) = spread(refs, 1, experts)
    wide = gate_up[0].shape[0] // 2
    for k in range(experts):
        acts[2 * k * wide : 2 * (k + 1) * wide, :] = dot_nt(gate_up[k][...], x[...])


def far_kernel(experts, slabs, ks, split, *refs):
    (acts,), down, xs, dys, both, hid, outs = spread(
        refs, 1, experts, slabs, slabs, slabs - 1, slabs - 1
    )
    (last, last_hid), grads = spread(outs, 2)
    rows, wide = xs[0].shape[0], down[0].shape[0]
    weights = weights_of(dys[-1], experts, rows, down[0].shape[1])
    for k in range(experts):
        back = back_of(down[k], dys[-1], rows)
        gate_act = acts[2 * k * wide : (2 * k + 1) * wide, :]
        up_act = acts[(2 * k + 1) * wide : (2 * k + 2) * wide, :]
        gate_grad, up_grad, weighted = grads_of(gate_act, up_act, back, weights[k])
        last[2 * k * wide : (2 * k + 1) * wide, :] = gate_grad
        last[(2 * k + 1) * wide : (2 * k + 2) * wide, :] = up_grad
        last_hid[k * wide : (k + 1) * wide, :] = weighted
    put_weight_grads(ks, split, xs, dys, (*both, last), (*hid, last_hid), grads)


def grads_kernel(slabs, ks, *refs):
    xs, dys, both, hid, grads = spread(refs, slabs, slabs, slabs, slabs)
    put_weight_grads(ks, (), xs, dys, both, hid, grads)


def near_kernel(experts, slabs, ks, *refs):
    gate_up, xs, dys, both, hid, outs = spread(refs, experts, slabs, slabs, slabs, slabs)
    (contrib,), grads = spread(outs, 1)
    put_weight_grads(ks, (), xs, dys, both, hid, grads)
    put_contrib(both[-1], gate_up, contrib)


def shape(rows, cols, kind=BF16):
    return jax.ShapeDtypeStruct((rows, cols), kind)


def after(value, *others):
    return lax.optimization_barrier((value, *others))[0] if others else value


def body(tokens, route_ids, route_probs, cotangent, w_gate_up, w_down):
    turns = lax.axis_size("dp")
    experts = lax.axis_size("expert")
    here = lax.axis_index("expert")
    wide, width = w_down.shape[1:]
    names = jnp.arange(experts, dtype=jnp.int32) ^ here

    rows = tokens.shape[0]
    prob = jnp.sum(
        jnp.where(route_ids[None] == names[:, None, None], route_probs[None], 0), axis=2
    ).astype(BF16)
    xs, dys = [tokens], [travelling(cotangent, prob)]
    for _ in range(turns - 1):
        xs.append(onward(xs[-1]))
        dys.append(onward(dys[-1]))
    gate_up = all_experts(after(w_gate_up, prob).reshape(2 * wide, width))
    down = all_experts(w_down.reshape(wide, width))

    slabs, units = len(xs), experts * wide
    both, hid, contrib = [], [], []
    for x, dyp in zip(xs[:-1], dys):
        b, h, c = call(
            functools.partial(slab_kernel, experts),
            (shape(2 * units, rows), shape(units, rows), shape(rows, width)),
            x, dyp, *gate_up, *down,
            cost=COSTS["slab"],
        )
        both.append(b)
        hid.append(h)
        contrib.append(c)
    (acts,) = call(
        functools.partial(acts_kernel, experts),
        (shape(2 * units, rows, F32),),
        xs[-1], *gate_up,
        cost=COSTS["acts"],
    )

    far = tuple(range(experts // 2, experts))[::-1]
    near = tuple(range(experts // 2))[::-1]
    split = tuple(k for k in far if k % 2)
    even = tuple(k for k in far if not k % 2)
    whole, third = shape(3 * wide, width), shape(wide, width)
    b, h, *got_split = call(
        functools.partial(far_kernel, experts, slabs, split, split),
        (shape(2 * units, rows), shape(units, rows), *[third] * (3 * len(split))),
        acts, *down, *xs, *dys, *both, *hid,
        cost=COSTS["far"],
    )
    both.append(b)
    hid.append(h)
    got_even = call(
        functools.partial(grads_kernel, slabs, even),
        [whole] * len(even),
        *xs, *dys, *both, *hid,
        cost=COSTS["even"],
    )
    got_far = []
    for k in far:
        if k in split:
            got_far, got_split = [*got_far, *got_split[:3]], got_split[3:]
        else:
            got_far, got_even = [*got_far, got_even[0]], got_even[1:]
    terms = {}
    for k in far:
        count = 3 if k in split else 1
        terms[k], got_far = [tuple(got_far[:count])], got_far[count:]
    first_bit, *other_bits = bits_of(experts)

    def swap_out(ks, bit):
        for k in ks:
            out = terms.pop(k)
            if len(out) > 1:
                out = [summed(out, [whole])]
                joined.extend(out[0])
            terms.setdefault(k ^ bit, []).append(tuple(swapped(v, bit) for v in out[0]))

    joined = []
    swap_out(split, first_bit)
    if len(other_bits) == 1:
        out = summed(terms.pop(even[0]), [whole], COSTS["join"])
        joined.extend(out)
        terms[0] = [(swapped(out[0], other_bits[0]),)]
    c, *got_near = call(
        functools.partial(near_kernel, experts, slabs, near),
        (shape(rows, width), *[whole] * len(near)),
        *gate_up, *xs, *dys, *both[:-1], after(both[-1], *joined), *hid,
        cost=COSTS["near"],
    )
    contrib.append(c)
    for k, got in zip(near, got_near):
        terms.setdefault(k, []).insert(0, (got,))
    back = [onward(after(contrib[1], *joined), -1)] if slabs > 1 else []
    acc = None
    if slabs > 2:
        acc = onward(after(contrib[2], acts))
    if acc is not None and joined:
        acc = after(acc, *joined)
    swap_out([k for k in near if k % 2], first_bit)
    if len(other_bits) != 1:
        for bit in other_bits:
            swap_out(sorted((k for k in terms if k & bit), reverse=True), bit)
    for i in range(3, slabs):
        (acc,) = summed([(acc,), (contrib[i],)], [shape(rows, width)], COSTS["add"])
        acc = onward(acc)
    tokens_terms = [contrib[0], *back, *([acc] if slabs > 2 else [])]
    acc, grad_gate_up, grad_down = finished(
        [tokens_terms, [t for (t,) in terms[0]]],
        [shape(rows, width), shape(2 * wide, width, F32), shape(wide, width, F32)],
        COSTS["last"],
    )
    return acc, grad_gate_up.reshape(1, 2, wide, width), grad_down.reshape(1, wide, width)


def solution(mesh):
    placed = (
        P(("groups", "expert", "dp"), None),
        P(("groups", "expert", "dp"), None),
        P(("groups", "expert", "dp"), None),
        P(("groups", "expert", "dp"), None),
        P("expert", None, "dp", None),
        P("expert", "dp", None),
    )
    return jax.shard_map(
        body,
        mesh=mesh,
        in_specs=placed,
        out_specs=(
            P(("groups", "expert", "dp"), None),
            P(("groups", "expert"), None, "dp", None),
            P(("groups", "expert"), "dp", None),
        ),
        check_vma=False,
    )
```

```python
import functools
import math

import jax
import jax.numpy as jnp
from jax import lax
from jax.experimental import pallas as pl
from jax.experimental.pallas import tpu as pltpu
from jax.sharding import PartitionSpec as P

BF16 = jnp.bfloat16
COSTS = {"slab": 2, "acts": 4, "far": 1, "even": 5, "near": 2, "join": 1, "add": 8, "last": 2}
F32 = jnp.float32


def ring_pairs(count, turns):
    order = [0] + list(range(1, count, 2)) + list(range(2, count, 2))[::-1]
    return [(order[i], order[(i + turns) % count]) for i in range(count)]


def onward(block, turns=1):
    return lax.ppermute(block, "dp", ring_pairs(lax.axis_size("dp"), turns))


def swapped(block, bit):
    return lax.ppermute(block, "expert", [(i, i ^ bit) for i in range(lax.axis_size("expert"))])


def bits_of(count):
    return [1 << i for i in range(count.bit_length() - 1)]


def all_experts(block):
    held = {0: block}
    for bit in bits_of(lax.axis_size("expert"))[::-1]:
        held.update({k | bit: swapped(v, bit) for k, v in list(held.items())})
    return [held[k] for k in range(len(held))]


def call(kernel, outs, *args, cost=0.0, scratch=()):
    return pl.pallas_call(
        kernel,
        out_shape=list(outs),
        in_specs=[pl.BlockSpec(memory_space=pltpu.VMEM)] * len(args),
        out_specs=[pl.BlockSpec(memory_space=pltpu.VMEM)] * len(outs),
        scratch_shapes=list(scratch),
        compiler_params=pltpu.CompilerParams(vmem_limit_bytes=40 * 1024 * 1024),
        cost_estimate=pl.CostEstimate(flops=int(cost * 1e9), bytes_accessed=0, transcendentals=0),
    )(*args)


def dot_nt(a, b):
    return lax.dot_general(a, b, (((1,), (1,)), ((), ())), preferred_element_type=F32)


def dot_tn(a, b):
    return lax.dot_general(a, b, (((0,), (0,)), ((), ())), preferred_element_type=F32)


def dot_nn(a, b):
    return jnp.dot(a, b, preferred_element_type=F32)


def grads_of(gate_act, up_act, back, weight):
    sigma = jax.nn.sigmoid(gate_act)
    silu_gate = gate_act * sigma
    weighted = weight * silu_gate * up_act
    back = weight * back
    gate_grad = back * up_act * sigma * (1.0 + gate_act * (1.0 - sigma))
    return gate_grad.astype(BF16), (back * silu_gate).astype(BF16), weighted.astype(BF16)


def spread(refs, *counts):
    at, groups = 0, []
    for count in counts:
        groups.append(refs[at : at + count])
        at += count
    return *groups, refs[at:]


def put_contrib(both, gate_up, contrib):
    wide2, width = gate_up[0].shape
    step = min(512, width)
    for at in range(0, width, step):
        cols = slice(at, at + step)
        total = None
        for k, block in enumerate(gate_up):
            term = dot_tn(rows_of(both, k, wide2), block[:, cols])
            total = term if total is None else total + term
        contrib[:, cols] = total.astype(BF16)


def put_weight_grads(ks, split, xs, dys, both, hid, outs):
    rows, width = xs[0].shape
    block = dys[0].shape[1]
    for k in ks:
        mine, outs = (outs[:3], outs[3:]) if k in split else (outs[:1], outs[1:])
        wide = sum(o.shape[0] for o in mine) // 3
        left_x = jnp.concatenate([rows_of(a, k, 2 * wide) for a in both], axis=1)
        left_dy = jnp.concatenate([rows_of(a, k, wide) for a in hid], axis=1)
        for n in range(width // block):
            cols = slice(n * block, (n + 1) * block)
            right_x = jnp.concatenate([x[:, cols] for x in xs], axis=0)
            right_dy = jnp.concatenate([dy[n * rows : (n + 1) * rows, :] for dy in dys], axis=0)
            got_x = dot_nn(left_x, right_x).astype(BF16)
            got_dy = dot_nn(left_dy, right_dy).astype(BF16)
            if len(mine) == 1:
                mine[0][: 2 * wide, cols] = got_x
                mine[0][2 * wide :, cols] = got_dy
            else:
                mine[0][:, cols] = got_x[:wide]
                mine[1][:, cols] = got_x[wide:]
                mine[2][:, cols] = got_dy


def sum_kernel(counts, *refs):
    parts, outs = [], refs[sum(counts) :]
    for count in counts:
        parts.append(refs[:count])
        refs = refs[count:]
    size = math.gcd(*(r.shape[0] for part in (*parts, outs) for r in part))

    def rows_at(part, at):
        for ref in part:
            if at < ref.shape[0]:
                return ref, slice(at, at + size)
            at -= ref.shape[0]

    for at in range(0, sum(r.shape[0] for r in outs), size):
        total = None
        for part in parts:
            ref, rows = rows_at(part, at)
            term = ref[rows, :].astype(F32)
            total = term if total is None else total + term
        ref, rows = rows_at(outs, at)
        ref[rows, :] = total.astype(ref.dtype)


def finish_kernel(counts, *refs):
    groups, refs = [refs[: counts[0]], refs[counts[0] : sum(counts)]], refs[sum(counts) :]
    outs, held, sems = refs[: len(refs) // 2], refs[len(refs) // 2 : -1], refs[-1]
    copies, first = [], [0, 0]
    for n, (out, buffer) in enumerate(zip(outs, held)):
        group = min(n, 1)
        height = out.shape[0]
        rows = height // 4 if height % 64 == 0 else height // 2
        for at in range(0, height, rows):
            step = 16 if rows % 16 == 0 else rows
            for low in range(0, rows, step):
                total = None
                for ref in groups[group]:
                    term = ref[first[group] + low : first[group] + low + step, :].astype(F32)
                    total = term if total is None else total + term
                buffer[at + low : at + low + step, :] = total.astype(buffer.dtype)
            copy = pltpu.make_async_copy(
                buffer.at[at : at + rows, :], out.at[at : at + rows, :], sems.at[len(copies)]
            )
            copy.start()
            copies.append(copy)
            first[group] += rows
    for copy in copies:
        copy.wait()


def finished(groups, outs, cost):
    args = [r for group in groups for r in group]
    return pl.pallas_call(
        functools.partial(finish_kernel, tuple(len(g) for g in groups)),
        out_shape=list(outs),
        in_specs=[pl.BlockSpec(memory_space=pltpu.VMEM)] * len(args),
        out_specs=[pl.BlockSpec(memory_space=pl.ANY)] * len(outs),
        scratch_shapes=[
            *[pltpu.VMEM(o.shape, o.dtype) for o in outs],
            pltpu.SemaphoreType.DMA((4 * len(outs),)),
        ],
        compiler_params=pltpu.CompilerParams(vmem_limit_bytes=40 * 1024 * 1024),
        cost_estimate=pl.CostEstimate(flops=int(cost * 1e9), bytes_accessed=0, transcendentals=0),
    )(*args)


def summed(addends, outs, cost=0.0):
    counts = tuple(len(a) for a in addends)
    return call(functools.partial(sum_kernel, counts), outs, *(r for a in addends for r in a), cost=cost)


def travelling(dy, prob):
    rows, width = dy.shape
    block = 2 * rows if width % (2 * rows) == 0 else width
    stacked = dy.reshape(rows, width // block, block).transpose(1, 0, 2).reshape(-1, block)
    below = -(-prob.size // (16 * block)) * 16
    packed = jnp.zeros((below * block,), BF16).at[: prob.size].set(prob.reshape(-1))
    return jnp.concatenate([stacked, packed.reshape(below, block)])


def weights_of(dyp, experts, rows, width):
    block = dyp.shape[1]
    per = block // rows
    packed = dyp[width // block * rows :, :].astype(F32)
    return [
        packed[k // per : k // per + 1, k % per * rows : (k % per + 1) * rows] for k in range(experts)
    ]


def rows_of(terms, k, size):
    if not isinstance(terms, tuple):
        return terms[k * size : (k + 1) * size, :]
    rest, some, names = terms
    if k in names:
        return rows_of(some, names.index(k), size)
    return rows_of(rest, k - sum(n < k for n in names), size)


def back_of(down, dyp, rows):
    block = dyp.shape[1]
    total = None
    for n in range(down.shape[1] // block):
        term = dot_nt(down[:, n * block : (n + 1) * block], dyp[n * rows : (n + 1) * rows, :])
        total = term if total is None else total + term
    return total


def slab_kernel(experts, *refs):
    (x, dyp), gate_up, down, (both, hid, contrib) = spread(refs, 2, experts, experts)
    rows, wide = x.shape[0], down[0].shape[0]
    weights = weights_of(dyp, experts, rows, x.shape[1])
    for k in range(experts):
        acts = dot_nt(gate_up[k][...], x[...])
        back = back_of(down[k], dyp, rows)
        gate_grad, up_grad, weighted = grads_of(acts[:wide], acts[wide:], back, weights[k])
        both[2 * k * wide : (2 * k + 1) * wide, :] = gate_grad
        both[(2 * k + 1) * wide : (2 * k + 2) * wide, :] = up_grad
        hid[k * wide : (k + 1) * wide, :] = weighted
    put_contrib(both, gate_up, contrib)


def acts_kernel(experts, *refs):
    (x,), gate_up, (acts,) = spread(refs, 1, experts)
    wide = gate_up[0].shape[0] // 2
    for k in range(experts):
        acts[2 * k * wide : 2 * (k + 1) * wide, :] = dot_nt(gate_up[k][...], x[...])


def put_last(ks, experts, rows, acts, down, dy, both, hid):
    wide = down[0].shape[0]
    weights = weights_of(dy, experts, rows, down[0].shape[1])
    for n, k in enumerate(ks):
        back = back_of(down[n], dy, rows)
        gate_act = acts[2 * k * wide : (2 * k + 1) * wide, :]
        up_act = acts[(2 * k + 1) * wide : (2 * k + 2) * wide, :]
        gate_grad, up_grad, weighted = grads_of(gate_act, up_act, back, weights[k])
        both[2 * n * wide : (2 * n + 1) * wide, :] = gate_grad
        both[(2 * n + 1) * wide : (2 * n + 2) * wide, :] = up_grad
        hid[n * wide : (n + 1) * wide, :] = weighted


def far_kernel(experts, slabs, split, *refs):
    (acts,), down, xs, dys, both, hid, outs = spread(
        refs, 1, len(split), slabs, slabs, slabs - 1, slabs - 1
    )
    (last, last_hid), grads = spread(outs, 2)
    put_last(split, experts, xs[0].shape[0], acts, down, dys[-1], last, last_hid)
    put_weight_grads(
        split, split, xs, dys,
        (*both, (None, last, split)), (*hid, (None, last_hid, split)), grads,
    )


def rest_kernel(experts, slabs, ks, rest, *refs):
    (acts,), down, xs, dys, both, hid, outs = spread(
        refs, 1, len(rest), slabs, slabs, slabs - 1, slabs - 1
    )
    (last, last_hid), grads = spread(outs, 2)
    put_last(rest, experts, xs[0].shape[0], acts, down, dys[-1], last, last_hid)
    names = tuple(k for k in range(experts) if k not in rest)
    put_weight_grads(
        ks, (), xs, dys, (*both, (last, None, names)), (*hid, (last_hid, None, names)), grads
    )


def near_kernel(experts, slabs, ks, split, *refs):
    gate_up, xs, dys, both, hid, outs = spread(refs, experts, slabs, slabs, slabs + 1, slabs + 1)
    (contrib,), grads = spread(outs, 1)
    both = (*both[:-2], (both[-2], both[-1], split))
    hid = (*hid[:-2], (hid[-2], hid[-1], split))
    put_weight_grads(ks, (), xs, dys, both, hid, grads)
    put_contrib(both[-1], gate_up, contrib)


def shape(rows, cols, kind=BF16):
    return jax.ShapeDtypeStruct((rows, cols), kind)


def after(value, *others):
    return lax.optimization_barrier((value, *others))[0] if others else value


def body(tokens, route_ids, route_probs, cotangent, w_gate_up, w_down):
    turns = lax.axis_size("dp")
    experts = lax.axis_size("expert")
    here = lax.axis_index("expert")
    wide, width = w_down.shape[1:]
    names = jnp.arange(experts, dtype=jnp.int32) ^ here

    rows = tokens.shape[0]
    prob = jnp.sum(
        jnp.where(route_ids[None] == names[:, None, None], route_probs[None], 0), axis=2
    ).astype(BF16)
    xs, dys = [tokens], [travelling(cotangent, prob)]
    for _ in range(turns - 1):
        xs.append(onward(xs[-1]))
        dys.append(onward(dys[-1]))
    gate_up = all_experts(after(w_gate_up, prob).reshape(2 * wide, width))
    down = all_experts(w_down.reshape(wide, width))

    slabs, units = len(xs), experts * wide
    both, hid, contrib = [], [], []
    for x, dyp in zip(xs[:-1], dys):
        b, h, c = call(
            functools.partial(slab_kernel, experts),
            (shape(2 * units, rows), shape(units, rows), shape(rows, width)),
            x, dyp, *gate_up, *down,
            cost=COSTS["slab"],
        )
        both.append(b)
        hid.append(h)
        contrib.append(c)
    (acts,) = call(
        functools.partial(acts_kernel, experts),
        (shape(2 * units, rows, F32),),
        xs[-1], *gate_up,
        cost=COSTS["acts"],
    )

    far = tuple(range(experts // 2, experts))[::-1]
    near = tuple(range(experts // 2))[::-1]
    split = tuple(k for k in range(experts // 2, experts) if k % 2)
    even = tuple(k for k in far if not k % 2)
    rest = tuple(k for k in range(experts) if k not in split)
    whole, third = shape(3 * wide, width), shape(wide, width)

    def last_terms(ks):
        return shape(2 * len(ks) * wide, rows), shape(len(ks) * wide, rows)

    b, h, *got_split = call(
        functools.partial(far_kernel, experts, slabs, split),
        (*last_terms(split), *[third] * (3 * len(split))),
        acts, *(down[k] for k in split), *xs, *dys, *both, *hid,
        cost=COSTS["far"],
    )
    b_rest, h_rest, *got_even = call(
        functools.partial(rest_kernel, experts, slabs, even, rest),
        (*last_terms(rest), *[whole] * len(even)),
        acts, *(down[k] for k in rest), *xs, *dys, *both, *hid,
        cost=COSTS["even"],
    )
    both += [b_rest, b]
    hid += [h_rest, h]
    got_split = dict(zip(split, zip(got_split[::3], got_split[1::3], got_split[2::3])))
    got_even = dict(zip(even, got_even))
    terms = {k: [got_split[k]] if k in split else [(got_even[k],)] for k in far}
    first_bit, *other_bits = bits_of(experts)

    def swap_out(ks, bit):
        for k in ks:
            out = terms.pop(k)
            if len(out) > 1:
                out = [summed(out, [whole])]
                joined.extend(out[0])
            terms.setdefault(k ^ bit, []).append(tuple(swapped(v, bit) for v in out[0]))

    joined = []
    swap_out(split, first_bit)
    if len(other_bits) == 1:
        out = summed(terms.pop(even[0]), [whole], COSTS["join"])
        joined.extend(out)
        terms[0] = [(swapped(out[0], other_bits[0]),)]
    c, *got_near = call(
        functools.partial(near_kernel, experts, slabs, near, split),
        (shape(rows, width), *[whole] * len(near)),
        *gate_up, *xs, *dys, *both[:-1], after(both[-1], *joined), *hid,
        cost=COSTS["near"],
    )
    contrib.append(c)
    for k, got in zip(near, got_near):
        terms.setdefault(k, []).insert(0, (got,))
    back = [onward(after(contrib[1], *joined), -1)] if slabs > 1 else []
    acc = None
    if slabs > 2:
        acc = onward(after(contrib[2], acts))
    if acc is not None and joined:
        acc = after(acc, *joined)
    swap_out([k for k in near if k % 2], first_bit)
    if len(other_bits) != 1:
        for bit in other_bits:
            swap_out(sorted((k for k in terms if k & bit), reverse=True), bit)
    for i in range(3, slabs):
        (acc,) = summed([(acc,), (contrib[i],)], [shape(rows, width)], COSTS["add"])
        acc = onward(acc)
    tokens_terms = [contrib[0], *back, *([acc] if slabs > 2 else [])]
    acc, grad_gate_up, grad_down = finished(
        [tokens_terms, [t for (t,) in terms[0]]],
        [shape(rows, width), shape(2 * wide, width, F32), shape(wide, width, F32)],
        COSTS["last"],
    )
    return acc, grad_gate_up.reshape(1, 2, wide, width), grad_down.reshape(1, wide, width)


def solution(mesh):
    placed = (
        P(("groups", "expert", "dp"), None),
        P(("groups", "expert", "dp"), None),
        P(("groups", "expert", "dp"), None),
        P(("groups", "expert", "dp"), None),
        P("expert", None, "dp", None),
        P("expert", "dp", None),
    )
    return jax.shard_map(
        body,
        mesh=mesh,
        in_specs=placed,
        out_specs=(
            P(("groups", "expert", "dp"), None),
            P(("groups", "expert"), None, "dp", None),
            P(("groups", "expert"), "dp", None),
        ),
        check_vma=False,
    )
```
